256 devices in a mesh: dp: 16 (over y_hi, x, core), seq: 16 (over z, y_lo).
Axes of the slice: x: 4, y: 4 (y_hi: 2, y_lo: 2; y = y_hi * 2 + y_lo), z: 8, core: 2. Of those that a mesh axis runs over, the one named last changes fastest.
Arguments:
- qkv: bfloat16 [2, 32768, 3, 2048], P(None, ('dp', 'seq')), may hold values from -100 to 100
- cotangent: bfloat16 [2, 32768, 1536], P(None, ('dp', 'seq')), may hold values from -6 to 6
- out_weight: bfloat16 [2048, 1536], P(('seq', 'dp')), may hold values from -0.125 to 0.125
- gate_table: float32 [50, 1536], replicated, may hold values from 0.25 to 2
- timestep: int32 [16], P('dp'), may hold values from 1 to 49
- plan: int32 [16, 16], P('dp'), may hold values from 0 to 1, as said below
Outputs:
- qkv_grad: bfloat16 [2, 32768, 3, 2048], P(None, ('dp', 'seq'))
- weight_grad: float32 [2048, 1536], P(('seq', 'dp'))
The draws below stay inside these ranges and needn't reach their ends.
Inputs may be any that keep to these rules, and one draw needn't show every extreme that they name: `plan`: in each clip exactly 12 frames are 1, the others 0.
All inputs are finite; a program needn't handle non-finite values.
Results may differ from the reference program's by a relative error of at most 0.034.
Values may be sent and summed in bfloat16 or wider, within the bound.
No kernel may reach another device: no remote copies, remote signals or barrier semaphores. Data moves between devices by JAX's collectives and lax.ppermute only.
A program may use at most 128 MiB of HBM per device.

```python
import jax
import jax.numpy as jnp
from jax import lax

DOUT = 1536
HEADS = 32
HEAD_DIM = 64
FT = 128
SAMPLER_STEPS = 50
INNER = 2048
FRAMES = 16
CLIP_LEN = 2048
LIVE = 4
CLIPS = 16
TOKENS = 32768


def draw_qkv(key, part):
    key = jax.random.fold_in(key, 9)
    base_key = jax.random.fold_in(key, 0)
    shape = (2, CLIPS, CLIP_LEN, 3, HEADS * HEAD_DIM)
    values = jnp.clip(jax.random.normal(base_key, shape, jnp.float32), -4.0, 4.0)
    return values.reshape(2, CLIPS * CLIP_LEN, 3, HEADS * HEAD_DIM).astype(jnp.bfloat16)


def draw_plan(key, part):
    key = jax.random.fold_in(key, 5)
    keys = jax.random.split(key, CLIPS)
    order = jax.vmap(lambda single: jax.random.permutation(single, FRAMES))(keys)
    return (order >= FRAMES // 4).astype(jnp.int32)


def touch_ends(entries, key, low, largest):
    dims = entries.shape
    place = [jax.random.randint(jax.random.fold_in(key, axis), (), 0, dims[axis]) for axis in range(len(dims))]
    entries = entries.at[tuple(place)].set(low)
    longest = dims.index(max(dims))
    place[longest] = (place[longest] + 1) % dims[longest]
    return entries.at[tuple(place)].set(largest)


def levels(key, dims, cuts, least, top_value):
    level, own = 1.0, jax.random.fold_in(key, 6)
    for position, blocks in cuts:
        steps = jnp.exp(jax.random.uniform(jax.random.fold_in(own, position), (blocks,), jnp.float32, least / len(cuts), top_value / len(cuts)))
        level = level * jnp.repeat(steps, dims[position] // blocks).reshape([-1 if axis == position else 1 for axis in range(len(dims))])
    return level


def scatter_about(stream_key, extent, deviation, reach, pieces=(), kind=jnp.bfloat16):
    factor_of = levels(stream_key, extent, pieces, -0.22, 0.18) if pieces else 1.0
    drawn = jax.random.normal(stream_key, extent, jnp.float32) * deviation * factor_of
    return jnp.minimum(jnp.maximum(drawn, -reach), reach).astype(kind)


def setup_inputs(seed: int = 0) -> dict:
    key_of = jax.random.split(jax.random.key(seed), 7)
    qkv = draw_qkv(jax.random.fold_in(key_of[6], 71), 0)
    cotangent = scatter_about(key_of[1], (2, TOKENS, DOUT), 1.0, 6.0, ((1, 256),))
    out_weight = scatter_about(key_of[2], (INNER, DOUT), INNER ** -0.5, 0.125, ((0, 256),))
    gate_table = jnp.clip(jax.random.uniform(key_of[3], (SAMPLER_STEPS, DOUT), jnp.float32, 0.25, 2.0), 0.25, 2.0)
    timestep = touch_ends(jax.random.randint(key_of[4], (CLIPS,), 1, SAMPLER_STEPS), jax.random.fold_in(key_of[4], 1), 1, SAMPLER_STEPS - 1).astype(jnp.int32)
    plan = draw_plan(jax.random.fold_in(key_of[6], 71), 0)
    return {"qkv": qkv, "cotangent": cotangent, "out_weight": out_weight, "gate_table": gate_table, "timestep": timestep, "plan": plan}


def head_grads(queries, keys, values, grad_out, scale):
    def one_head(parts):
        query_h, key_h, value_h, grad_h = parts
        scores = jnp.dot(query_h, key_h.T, preferred_element_type=jnp.float32) * scale
        top = jnp.max(scores, axis=1, keepdims=True)
        expo = jnp.exp(scores - top)
        probs = expo / jnp.sum(expo, axis=1, keepdims=True)
        probs_low = probs.astype(jnp.bfloat16)
        output = jnp.dot(probs_low, value_h, preferred_element_type=jnp.float32).astype(jnp.bfloat16)
        grad_probs = jnp.dot(grad_h, value_h.T, preferred_element_type=jnp.float32)
        delta = jnp.sum(grad_h.astype(jnp.float32) * output.astype(jnp.float32), axis=1, keepdims=True)
        grad_scores = (probs * (grad_probs - delta)).astype(jnp.bfloat16)
        grad_q = (jnp.dot(grad_scores, key_h, preferred_element_type=jnp.float32) * scale).astype(jnp.bfloat16)
        grad_k = (jnp.dot(grad_scores.T, query_h, preferred_element_type=jnp.float32) * scale).astype(jnp.bfloat16)
        grad_v = jnp.dot(probs_low.T, grad_h, preferred_element_type=jnp.float32).astype(jnp.bfloat16)
        return output, grad_q, grad_k, grad_v

    heads_first = tuple(jnp.transpose(item, (1, 0, 2)) for item in (queries, keys, values, grad_out))
    results = lax.map(one_head, heads_first)
    return tuple(jnp.transpose(item, (1, 0, 2)) for item in results)


def reference(qkv, cotangent, out_weight, gate_table, timestep, plan):
    scale = HEAD_DIM ** -0.5
    clip_qkv = jnp.moveaxis(qkv.reshape(2, CLIPS, CLIP_LEN, 3, HEADS, HEAD_DIM), 1, 0)
    clip_cot = jnp.moveaxis(cotangent.reshape(2, CLIPS, CLIP_LEN, DOUT), 1, 0)

    def one_clip(total, parts):
        query_key_value_clip, cotangent_per_clip, time_now, flags = parts
        gate_now = lax.dynamic_index_in_dim(gate_table, time_now, 0, keepdims=False)
        gate_prev = lax.dynamic_index_in_dim(gate_table, time_now - 1, 0, keepdims=False)
        reuse = jnp.repeat(flags, FT).astype(jnp.float32)[:, None]
        grads_in = cotangent_per_clip.astype(jnp.float32)
        res_one = (gate_now * grads_in[0] + reuse * (gate_prev * grads_in[1])).astype(jnp.bfloat16)
        res_two = ((1.0 - reuse) * (gate_prev * grads_in[1])).astype(jnp.bfloat16)
        dout_one = jnp.dot(res_one, out_weight.T, preferred_element_type=jnp.float32).astype(jnp.bfloat16)
        dout_two = jnp.dot(res_two, out_weight.T, preferred_element_type=jnp.float32).astype(jnp.bfloat16)
        dout_one = dout_one.reshape(CLIP_LEN, HEADS, HEAD_DIM)
        dout_two = dout_two.reshape(CLIP_LEN, HEADS, HEAD_DIM)
        live = jnp.argsort(flags, stable=True)[:LIVE].astype(jnp.int32)
        rows = (live[:, None] * FT + jnp.arange(FT, dtype=jnp.int32)[None, :]).reshape(-1)
        out_one, dq_one, dk_one, dv_one = head_grads(query_key_value_clip[0, :, 0], query_key_value_clip[0, :, 1], query_key_value_clip[0, :, 2], dout_one, scale)
        out_two, dq_live, dk_two, dv_two = head_grads(query_key_value_clip[1, :, 0][rows], query_key_value_clip[1, :, 1], query_key_value_clip[1, :, 2], dout_two[rows], scale)
        dq_two = jnp.zeros_like(dq_one).at[rows].set(dq_live)
        grads = jnp.stack([jnp.stack([dq_one, dk_one, dv_one], axis=1), jnp.stack([dq_two, dk_two, dv_two], axis=1)])
        term = jnp.dot(out_one.reshape(CLIP_LEN, INNER).T, res_one, preferred_element_type=jnp.float32)
        term = term + jnp.dot(out_two.reshape(LIVE * FT, INNER).T, res_two[rows], preferred_element_type=jnp.float32)
        return total + term, grads.reshape(2, CLIP_LEN, 3, INNER)

    start = jnp.zeros((INNER, DOUT), jnp.float32)
    weight_grad, grads = lax.scan(one_clip, start, (clip_qkv, clip_cot, timestep, plan))
    qkv_grad = jnp.moveaxis(grads, 0, 1).reshape(2, TOKENS, 3, INNER)
    return qkv_grad, weight_grad
```

```python
import functools
import jax
import jax.numpy as jnp
from jax import lax
from jax.experimental import pallas as pl
from jax.experimental.pallas import tpu as pltpu
from jax.sharding import Mesh
from jax.sharding import PartitionSpec as P

HEAD_DIM = 64
FT = 128
KC = 256


def attn_kernel(rows_ref, x_ref, d_ref, o_ref, g_ref, dk_ref, dv_ref, kt_ref, vt_ref, s_ref, e_ref, *, frames, picked, scale):
    step = pl.program_id(0)
    length = frames * FT
    chunks = length // KC
    per = KC // FT
    width = 2 * HEAD_DIM
    block = d_ref.shape[0]

    @pl.when(step == 0)
    def _():
        dk_ref[...] = jnp.zeros_like(dk_ref)
        dv_ref[...] = jnp.zeros_like(dv_ref)
        for f in range(frames):
            kt_ref[:, f * FT:(f + 1) * FT] = x_ref[f, 1].T
            vt_ref[:, f * FT:(f + 1) * FT] = x_ref[f, 2].T
            if picked < frames:
                g_ref[f, 0] = jnp.zeros((FT, width), jnp.bfloat16)

    nb = block // FT
    own = [rows_ref[step * nb + j] for j in range(nb)]
    q = jnp.concatenate([x_ref[own[j], 0] for j in range(nb)], axis=0) * jnp.bfloat16(scale)
    do = d_ref[...]
    q_t = q.T
    do_t = do.T.astype(jnp.float32)
    lane = lax.broadcasted_iota(jnp.int32, (block, width), 1)
    sub = lax.broadcasted_iota(jnp.int32, (width, block), 0)
    zero_q = jnp.zeros_like(q)
    zero_t = jnp.zeros_like(q_t)
    f32 = jnp.float32

    def keys(which, c):
        return x_ref[c * per:(c + 1) * per, which].reshape(KC, width)

    deltas, do_scaled, outs = [], [], []
    for h in range(2):
        lo, hi = h * HEAD_DIM, (h + 1) * HEAD_DIM
        q_th = jnp.where((sub >= lo) & (sub < hi), q_t, zero_t)
        top = None
        for c in range(chunks):
            s = jnp.dot(keys(1, c), q_th, preferred_element_type=f32)
            s_ref[h, c * KC:(c + 1) * KC, :] = s
            part = jnp.max(s.reshape(KC // 8, 8, block), axis=0)
            top = part if top is None else jnp.maximum(top, part)
        top = jnp.max(top, axis=0, keepdims=True)
        total = jnp.zeros((8, block), f32)
        out_t = jnp.zeros((HEAD_DIM, block), f32)
        for c in range(chunks):
            e = jnp.exp(s_ref[h, c * KC:(c + 1) * KC, :] - top)
            total = total + jnp.sum(e.reshape(KC // 8, 8, block), axis=0)
            eb = e.astype(jnp.bfloat16)
            e_ref[h, c * KC:(c + 1) * KC, :] = eb
            out_t = out_t + jnp.dot(vt_ref[lo:hi, c * KC:(c + 1) * KC], eb, preferred_element_type=f32)
        inv = 1.0 / jnp.sum(total, axis=0, keepdims=True)
        out_b = (out_t * inv).astype(jnp.bfloat16)
        outs.append(out_b)
        scaled = (do_t[lo:hi] * inv).astype(jnp.bfloat16)
        do_scaled.append(scaled)
        deltas.append(jnp.sum(scaled.astype(f32) * out_b.astype(f32), axis=0, keepdims=True))
    o_ref[...] = jnp.concatenate(outs, axis=0).T
    ds_t = jnp.concatenate(do_scaled, axis=0)
    ds_row = ds_t.T
    dq_t = [jnp.zeros((HEAD_DIM, block), f32) for _ in range(2)]
    d_th = [jnp.where((sub >= h * HEAD_DIM) & (sub < (h + 1) * HEAD_DIM), ds_t, zero_t) for h in range(2)]
    d_row = [jnp.where((lane >= h * HEAD_DIM) & (lane < (h + 1) * HEAD_DIM), ds_row, zero_q) for h in range(2)]
    q_row = [jnp.where((lane >= h * HEAD_DIM) & (lane < (h + 1) * HEAD_DIM), q, zero_q) for h in range(2)]
    for c in range(chunks):
        rows = slice(c * KC, (c + 1) * KC)
        dk, dv = dk_ref[rows, :], dv_ref[rows, :]
        for h in range(2):
            lo, hi = h * HEAD_DIM, (h + 1) * HEAD_DIM
            dp = jnp.dot(keys(2, c), d_th[h], preferred_element_type=f32)
            eb = e_ref[h, rows, :]
            grad = (eb.astype(f32) * (dp - deltas[h])).astype(jnp.bfloat16)
            dq_t[h] = dq_t[h] + jnp.dot(kt_ref[lo:hi, rows], grad, preferred_element_type=f32)
            dk = dk + jnp.dot(grad, q_row[h], preferred_element_type=f32)
            dv = dv + jnp.dot(eb, d_row[h], preferred_element_type=f32)
        dk_ref[rows, :] = dk
        dv_ref[rows, :] = dv
    dq = (jnp.concatenate(dq_t, axis=0) * scale).astype(jnp.bfloat16).T
    for j in range(nb):
        g_ref[own[j], 0] = dq[j * FT:(j + 1) * FT]

    @pl.when(step == pl.num_programs(0) - 1)
    def _():
        for f in range(frames):
            g_ref[f, 1] = dk_ref[f * FT:(f + 1) * FT, :].astype(jnp.bfloat16)
            g_ref[f, 2] = dv_ref[f * FT:(f + 1) * FT, :].astype(jnp.bfloat16)


def attend(rows, heads, grads, block=256):
    frames, _, _, width = heads.shape
    picked = rows.shape[0]
    length = frames * FT
    whole = lambda i, r: (0, 0, 0, 0)
    kernel = functools.partial(attn_kernel, frames=frames, picked=picked, scale=HEAD_DIM ** -0.5)
    return pl.pallas_call(
        kernel,
        grid_spec=pltpu.PrefetchScalarGridSpec(
            num_scalar_prefetch=1,
            grid=(picked * FT // block,),
            in_specs=[
                pl.BlockSpec(heads.shape, whole),
                pl.BlockSpec((block, width), lambda i, r: (i, 0)),
            ],
            out_specs=[
                pl.BlockSpec((block, width), lambda i, r: (i, 0)),
                pl.BlockSpec(heads.shape, whole),
            ],
            scratch_shapes=[
                pltpu.VMEM((length, width), jnp.float32),
                pltpu.VMEM((length, width), jnp.float32),
                pltpu.VMEM((width, length), jnp.bfloat16),
                pltpu.VMEM((width, length), jnp.bfloat16),
                pltpu.VMEM((2, length, block), jnp.float32),
                pltpu.VMEM((2, length, block), jnp.bfloat16),
            ],
        ),
        out_shape=[
            jax.ShapeDtypeStruct((picked * FT, width), jnp.bfloat16),
            jax.ShapeDtypeStruct(heads.shape, jnp.bfloat16),
        ],
        compiler_params=pltpu.CompilerParams(vmem_limit_bytes=48 * 1024 * 1024),
        name="attend",
    )(rows, heads, grads)


def swap(value):
    return lax.ppermute(value, ("co", "yl"), [(0, 0), (1, 2), (2, 1), (3, 3)])


def live_frames(flags, count):
    frames = flags.shape[0]
    index = jnp.arange(frames, dtype=jnp.int32)
    free = flags == 0
    before = jnp.sum((index[None, :] < index[:, None]) & free[None, :], axis=1)
    hit = free[None, :] & (before[None, :] == jnp.arange(count, dtype=jnp.int32)[:, None])
    return jnp.sum(jnp.where(hit, index[None, :], 0), axis=1).astype(jnp.int32)


def split_heads(qkv_step, groups):
    tokens, three, inner = qkv_step.shape
    return jnp.transpose(qkv_step.reshape(tokens, three, groups, inner // groups), (2, 1, 0, 3))


def join_heads(blocks):
    groups, three, tokens, width = blocks.shape
    return jnp.transpose(blocks, (2, 1, 0, 3)).reshape(tokens, three, groups * width)


def per_device(qkv, cotangent, out_weight, gate_table, timestep, plan):
    seq, group = ("z", "yl"), ("co", "z")
    frames = lax.axis_size(seq)
    half = frames // 2
    live_count = frames // 4
    tokens, dout = cotangent.shape[1:]
    piece = tokens // frames
    gate_now = lax.dynamic_index_in_dim(gate_table, timestep[0], 0, keepdims=False)
    gate_prev = lax.dynamic_index_in_dim(gate_table, timestep[0] - 1, 0, keepdims=False)
    flags = plan[0]
    reuse = lax.dynamic_index_in_dim(flags, lax.axis_index(seq), 0, keepdims=False).astype(jnp.float32)
    live = live_frames(flags, live_count)
    grads_in = cotangent.astype(jnp.float32)
    res_one = (gate_now * grads_in[0] + reuse * (gate_prev * grads_in[1])).astype(jnp.bfloat16)
    res_two = ((1.0 - reuse) * (gate_prev * grads_in[1])).astype(jnp.bfloat16)

    heads_one = lax.all_to_all(split_heads(qkv[0], frames), seq, 0, 0, tiled=True)
    chunks = lax.all_to_all(res_two.reshape(frames, piece, dout), seq, 0, 0, tiled=True)
    chunks = chunks[live].reshape(live_count * piece, dout)
    rows = jnp.concatenate([res_one, chunks], axis=0)
    residual = lax.all_gather(swap(rows), group, axis=0)
    heads_two = lax.all_to_all(split_heads(qkv[1], frames), seq, 0, 0, tiled=True)
    weight = lax.all_gather(swap(out_weight), ("yh", "x", "yl"), axis=0, tiled=True)

    grad_rows = jnp.einsum(
        "rte,ke->rtk", residual, weight, preferred_element_type=jnp.float32
    ).astype(jnp.bfloat16)
    grad_rows = swap(grad_rows)
    width = grad_rows.shape[2]
    grad_one = jnp.swapaxes(grad_rows[:, :tokens].reshape(2, half, tokens, width), 0, 1)
    grad_two = grad_rows[:, tokens:].reshape(2, half, live_count, piece, width)
    grad_two = jnp.transpose(grad_two, (2, 1, 0, 3, 4))

    out_one, back_one = attend(
        jnp.arange(frames, dtype=jnp.int32), heads_one, grad_one.reshape(frames * tokens, width)
    )
    grads_one = lax.all_to_all(back_one, seq, 0, 0, tiled=True)
    out_two, back_two = attend(live, heads_two, grad_two.reshape(live_count * tokens, width))
    grads_two = lax.all_to_all(back_two, seq, 0, 0, tiled=True)

    out_one = jnp.swapaxes(out_one.reshape(half, 2, tokens, width), 0, 1)
    out_two = jnp.transpose(out_two.reshape(live_count, half, 2, piece, width), (2, 1, 0, 3, 4))
    outputs = jnp.concatenate(
        [out_one.reshape(frames, tokens, width), out_two.reshape(frames, live_count * piece, width)],
        axis=1,
    )
    outputs = swap(outputs)
    partial = jnp.einsum("rtk,rte->ke", outputs, residual, preferred_element_type=jnp.float32)
    parts = lax.all_to_all(
        partial.reshape(frames, width // frames, dout), ("yh", "x", "yl"), 0, 0, tiled=True
    )
    weight_grad = swap(jnp.sum(parts, axis=0))
    return jnp.stack([join_heads(grads_one), join_heads(grads_two)]), weight_grad


def solution(mesh):
    whole = Mesh(mesh.devices.reshape(2, 4, 2, 8, 2), ("yh", "x", "co", "z", "yl"))
    dp, seq = ("yh", "x", "co"), ("z", "yl")
    placed = (
        P(None, dp + seq, None, None),
        P(None, dp + seq, None),
        P(seq + dp, None),
        P(),
        P(dp),
        P(dp, None),
    )
    return jax.shard_map(
        per_device,
        mesh=whole,
        in_specs=placed,
        out_specs=(P(None, dp + seq, None, None), P(seq + dp, None)),
        check_vma=False,
    )
```

```python
import functools

import jax
import jax.numpy as jnp
from jax import lax
from jax.experimental import pallas as pl
from jax.experimental.pallas import tpu as pltpu
from jax.sharding import Mesh
from jax.sharding import PartitionSpec as P

HEAD_DIM = 64
FT = 128
KC = 1024
BLOCK = 256
WIDTH = 2 * HEAD_DIM
MIB = 1024 * 1024
PARAMS = pltpu.CompilerParams(vmem_limit_bytes=16 * MIB)
ATTEND_PARAMS = pltpu.CompilerParams(vmem_limit_bytes=20 * MIB)
RESIDENT = pl.BlockSpec(memory_space=pltpu.VMEM)
SMALL = pl.CostEstimate(flops=1000, transcendentals=0, bytes_accessed=1000)
F32 = jnp.float32
LOW = jnp.bfloat16


def prepare_kernel(time_ref, flags_ref, pos_ref, qkv_ref, cot_ref, gate_ref, sent_ref, one_ref):
    frames = sent_ref.shape[0]
    tokens, dout = one_ref.shape
    now = gate_ref[pl.ds(time_ref[0], 1), :]
    prev = gate_ref[pl.ds(time_ref[0] - 1, 1), :]
    reuse = flags_ref[pos_ref[0]].astype(F32)
    second = prev * cot_ref[1].astype(F32)
    one_ref[...] = (now * cot_ref[0].astype(F32) + reuse * second).astype(LOW)
    second = (1.0 - reuse) * second
    size = tokens // frames
    for f in range(frames):
        for w in range(3):
            sent_ref[f, w * FT:(w + 1) * FT, :] = qkv_ref[0, w, :, f * WIDTH:(f + 1) * WIDTH]
        rows = second[f * size:(f + 1) * size]
        parts = [rows[:, j * WIDTH:(j + 1) * WIDTH] for j in range(dout // WIDTH)]
        sent_ref[f, 3 * FT:, :] = jnp.concatenate(parts, axis=0).astype(LOW)


def prepare(timestep, flags, position, qkv, cotangent, gates, frames):
    _, three, tokens, inner = qkv.shape
    dout = cotangent.shape[2]
    sent = (frames, three * tokens + tokens * dout // frames // WIDTH, WIDTH)
    return pl.pallas_call(
        prepare_kernel,
        grid_spec=pltpu.PrefetchScalarGridSpec(
            num_scalar_prefetch=3,
            grid=(1,),
            in_specs=[
                pl.BlockSpec((1, three, tokens, inner), lambda *_: (1, 0, 0, 0)),
                RESIDENT,
                RESIDENT,
            ],
            out_specs=[RESIDENT, RESIDENT],
        ),
        out_shape=[
            jax.ShapeDtypeStruct(sent, LOW),
            jax.ShapeDtypeStruct((tokens, dout), LOW),
        ],
        compiler_params=PARAMS,
        cost_estimate=SMALL,
        name="prepare",
    )(timestep, flags, position, qkv, cotangent, gates)


def call_on(kernel, operands, shapes, dtype, name):
    count = len(operands)

    def body(*refs):
        kernel(refs[:count], refs[count:])

    return pl.pallas_call(
        body,
        in_specs=[RESIDENT] * count,
        out_specs=[RESIDENT] * len(shapes),
        out_shape=[jax.ShapeDtypeStruct(shape, dtype) for shape in shapes],
        compiler_params=PARAMS,
        cost_estimate=SMALL,
        name=name,
    )(*operands)


def first_pieces(refs):
    first, f1, f2, f3, f4, b1, b2, b3, b4 = refs
    rows = first.shape[0]
    far = jnp.concatenate([f4[...], b4[...]], axis=0)
    return [first[...], f1[...], f2[:rows], f3[:rows], far, b3[:rows], b2[:rows], b1[...]]


def second_pieces(refs, rows):
    second, f2, f3, f4, f5, b2, b3, b4, b5 = refs
    far = jnp.concatenate([f5[...], b5[...]], axis=0)
    return [second[...], f2[rows:], f3[rows:], f4[...], far, b4[...], b3[rows:], b2[rows:]]


def project(weight, other, ring, pieces_of):
    def kernel(held, outs):
        rows = jnp.concatenate([held[0][...], held[1][...]], axis=0)
        for j, piece in enumerate(pieces_of(held[2:])):
            got = lax.dot_general(piece, rows, (((1,), (1,)), ((), ())), preferred_element_type=F32)
            got = got.astype(LOW)
            for k in range(2):
                outs[k][j] = got[:, k * WIDTH:(k + 1) * WIDTH]

    shape = (lax.axis_size("z"), ring[0].shape[0], WIDTH)
    return call_on(kernel, [weight, other, *ring], [shape] * 2, LOW, "project")


def outer(outputs, ring_one, ring_two):
    count = len(ring_one)

    def kernel(held, outs):
        one = first_pieces(held[4:4 + count])
        two = second_pieces(held[4 + count:], held[4].shape[0])
        rows = jnp.concatenate(one + two, axis=0)
        for k in range(2):
            left = [held[k][...].reshape(-1, WIDTH), held[2 + k][...].reshape(-1, WIDTH)]
            left = jnp.concatenate(left, axis=0).T
            outs[k][...] = jnp.dot(left, rows, preferred_element_type=F32)

    shape = (WIDTH, ring_one[0].shape[1])
    return call_on(kernel, [*outputs, *ring_one, *ring_two], [shape] * 2, F32, "outer")


def split_kernel(qkv_ref, sent_ref):
    for f in range(sent_ref.shape[0]):
        for w in range(3):
            sent_ref[f, w * FT:(w + 1) * FT, :] = qkv_ref[0, w, :, f * WIDTH:(f + 1) * WIDTH]


def split_heads(qkv, step, frames):
    _, three, tokens, inner = qkv.shape
    sent = (frames, three * tokens, WIDTH)
    return pl.pallas_call(
        split_kernel,
        grid=(1,),
        in_specs=[pl.BlockSpec((1, three, tokens, inner), lambda i: (step, 0, 0, 0))],
        out_specs=RESIDENT,
        out_shape=jax.ShapeDtypeStruct(sent, LOW),
        compiler_params=PARAMS,
        cost_estimate=SMALL,
        name="split_heads",
    )(qkv)


def join_kernel(back_ref, *refs):
    out_ref = refs[-1]
    for f in range(back_ref.shape[0]):
        for w in range(3):
            out_ref[0, w, :, f * WIDTH:(f + 1) * WIDTH] = back_ref[f, w * FT:(w + 1) * FT, :]


def join_heads(back, step, held=None):
    frames, rows, width = back.shape
    shape = (2, 3, rows // 3, frames * width)
    specs, operands, aliases = [RESIDENT], [back], {}
    if held is not None:
        specs.append(pl.BlockSpec(memory_space=pl.ANY))
        operands.append(held)
        aliases = {1: 0}
    return pl.pallas_call(
        join_kernel,
        grid=(1,),
        in_specs=specs,
        out_specs=pl.BlockSpec((1,) + shape[1:], lambda i: (step, 0, 0, 0)),
        out_shape=jax.ShapeDtypeStruct(shape, LOW),
        input_output_aliases=aliases,
        compiler_params=PARAMS,
        cost_estimate=SMALL,
        name="join_heads",
    )(*operands)


def live_rows(rows_ref, at, size, live, back):
    count = live * FT
    place, low = rows_ref[live], rows_ref[live + 1]
    row = lax.broadcasted_iota(jnp.int32, (size, count), 0) + at
    col = lax.broadcasted_iota(jnp.int32, (size, count), 1)
    straight, ringed = (col, row) if back else (row, col)
    part = lax.rem(ringed, 8)
    frame = lax.rem(lax.div(ringed, 8), live)
    turn_by = lax.rem(lax.div(ringed, 8 * live), 8)
    side = lax.div(ringed, 64 * live)
    eighth = lax.rem(turn_by + place, 8)
    side = side + low - 2 * side * low
    return (straight == frame * FT + eighth * 16 + side * 8 + part).astype(F32).astype(LOW)


def attend_kernel(
    rows_ref, x_ref, d_ref, f_ref, o_ref, p_ref, g_ref, dk_ref, dv_ref, kt_ref, vt_ref, s_ref, e_ref,
    all_ref, *, scale, by_frame
):
    step = pl.program_id(0)
    frames, width = x_ref.shape[0], x_ref.shape[2]
    chunks = frames * FT // KC
    per, nb = KC // FT, BLOCK // FT

    @pl.when(step == 0)
    def _():
        dk_ref[...] = jnp.zeros_like(dk_ref)
        dv_ref[...] = jnp.zeros_like(dv_ref)
        for f in range(frames):
            kt_ref[:, f * FT:(f + 1) * FT] = x_ref[f, FT:2 * FT].T
            vt_ref[:, f * FT:(f + 1) * FT] = x_ref[f, 2 * FT:3 * FT].T
            if not by_frame:
                g_ref[f, 0:FT] = jnp.zeros((FT, width), LOW)

    own = [rows_ref[step * nb + j] for j in range(nb)]
    q = jnp.concatenate([x_ref[own[j], 0:FT] for j in range(nb)], axis=0) * LOW(scale)
    if by_frame:
        do = jnp.concatenate([d_ref[0], f_ref[0]], axis=0)
    else:
        live = rows_ref.shape[0] - 2
        ringed = [r[...].reshape(-1, width) for r in (d_ref, f_ref)]
        pick = live_rows(rows_ref, step * BLOCK, BLOCK, live, False)
        do = jnp.dot(pick, jnp.concatenate(ringed, axis=0), preferred_element_type=F32).astype(LOW)
    q_t = q.T
    do_t = do.T.astype(F32)
    lane = lax.broadcasted_iota(jnp.int32, (BLOCK, width), 1)
    sub = lax.broadcasted_iota(jnp.int32, (width, BLOCK), 0)
    zero, zero_t = jnp.zeros_like(q), jnp.zeros_like(q_t)
    in_lanes = [(lane >= h * HEAD_DIM) & (lane < (h + 1) * HEAD_DIM) for h in range(2)]
    in_subs = [(sub >= h * HEAD_DIM) & (sub < (h + 1) * HEAD_DIM) for h in range(2)]

    def part_of(which, c):
        return x_ref[c * per:(c + 1) * per, which * FT:(which + 1) * FT].reshape(KC, width)

    def fold(value):
        return value.reshape(value.shape[0] // 8, 8, value.shape[1])

    deltas, scaled, outs = [], [], []
    for h in range(2):
        lo, hi = h * HEAD_DIM, (h + 1) * HEAD_DIM
        q_th = jnp.where(in_subs[h], q_t, zero_t)
        top = None
        for c in range(chunks):
            s = jnp.dot(part_of(1, c), q_th, preferred_element_type=F32)
            s_ref[h, c * KC:(c + 1) * KC, :] = s
            part = jnp.max(fold(s), axis=0)
            top = part if top is None else jnp.maximum(top, part)
        top = jnp.max(top, axis=0, keepdims=True)
        total = jnp.zeros((8, BLOCK), F32)
        out_t = jnp.zeros((HEAD_DIM, BLOCK), F32)
        for c in range(chunks):
            rows = slice(c * KC, (c + 1) * KC)
            e = jnp.exp(s_ref[h, rows, :] - top)
            total = total + jnp.sum(fold(e), axis=0)
            eb = e.astype(LOW)
            e_ref[h, rows, :] = eb
            out_t = out_t + jnp.dot(vt_ref[lo:hi, rows], eb, preferred_element_type=F32)
        inv = 1.0 / jnp.sum(total, axis=0, keepdims=True)
        out_b = (out_t * inv).astype(LOW)
        outs.append(out_b)
        part = (do_t[lo:hi] * inv).astype(LOW)
        scaled.append(part)
        deltas.append(jnp.sum(part.astype(F32) * out_b.astype(F32), axis=0, keepdims=True))
    out = jnp.concatenate(outs, axis=0).T
    if by_frame:
        o_ref[0] = out[0:FT]
        p_ref[0] = out[FT:]
    else:
        all_ref[pl.ds(pl.multiple_of(step * BLOCK, BLOCK), BLOCK), :] = out
    ds_t = jnp.concatenate(scaled, axis=0)
    ds_row = ds_t.T
    dq_t = [jnp.zeros((HEAD_DIM, BLOCK), F32) for _ in range(2)]
    d_th = [jnp.where(in_subs[h], ds_t, zero_t) for h in range(2)]
    d_row = [jnp.where(in_lanes[h], ds_row, zero) for h in range(2)]
    q_row = [jnp.where(in_lanes[h], q, zero) for h in range(2)]
    for c in range(chunks):
        rows = slice(c * KC, (c + 1) * KC)
        gs, es = [], []
        both = jnp.dot(part_of(2, c), jnp.concatenate(d_th, axis=1), preferred_element_type=F32)
        for h in range(2):
            lo, hi = h * HEAD_DIM, (h + 1) * HEAD_DIM
            dp = both[:, h * BLOCK:(h + 1) * BLOCK]
            eb = e_ref[h, rows, :]
            grad = (eb.astype(F32) * (dp - deltas[h])).astype(LOW)
            dq_t[h] = dq_t[h] + jnp.dot(kt_ref[lo:hi, rows], grad, preferred_element_type=F32)
            gs.append(grad)
            es.append(eb)
        dk = dk_ref[rows, :] + jnp.dot(jnp.concatenate(gs, axis=1), jnp.concatenate(q_row, axis=0), preferred_element_type=F32)
        dv = dv_ref[rows, :] + jnp.dot(jnp.concatenate(es, axis=1), jnp.concatenate(d_row, axis=0), preferred_element_type=F32)
        dk_ref[rows, :] = dk
        dv_ref[rows, :] = dv
    dq = (jnp.concatenate(dq_t, axis=0) * scale).astype(LOW).T
    for j in range(nb):
        g_ref[own[j], 0:FT] = dq[j * FT:(j + 1) * FT]

    @pl.when(step == pl.num_programs(0) - 1)
    def _():
        for f in range(frames):
            g_ref[f, FT:2 * FT] = dk_ref[f * FT:(f + 1) * FT, :].astype(LOW)
            g_ref[f, 2 * FT:3 * FT] = dv_ref[f * FT:(f + 1) * FT, :].astype(LOW)
        if not by_frame:
            half = live * FT // 2
            for k, ref in enumerate((o_ref, p_ref)):
                pick = live_rows(rows_ref, k * half, half, live, True)
                ringed = jnp.dot(pick, all_ref[...], preferred_element_type=F32).astype(LOW)
                ref[...] = ringed.reshape(ref.shape)


def attend(rows, heads, grads, live=0):
    frames, _, width = heads.shape
    length = frames * FT
    steps = (live or frames) * FT // BLOCK
    back = (frames, 3 * FT, width)
    outputs = grads[0].shape
    ring = outputs[0]
    if live:
        spec = RESIDENT
    else:
        spec = pl.BlockSpec(
            (1, FT, width), lambda i, r: (lax.rem(i + ring - r[frames], ring), 0, 0)
        )
    return pl.pallas_call(
        functools.partial(attend_kernel, scale=HEAD_DIM ** -0.5, by_frame=not live),
        grid_spec=pltpu.PrefetchScalarGridSpec(
            num_scalar_prefetch=1,
            grid=(steps,),
            in_specs=[RESIDENT, spec, spec],
            out_specs=[spec, spec, RESIDENT],
            scratch_shapes=[
                pltpu.VMEM((length, width), F32),
                pltpu.VMEM((length, width), F32),
                pltpu.VMEM((width, length), LOW),
                pltpu.VMEM((width, length), LOW),
                pltpu.VMEM((2, length, BLOCK), F32),
                pltpu.VMEM((2, length, BLOCK), LOW),
                pltpu.VMEM((max(live * FT, FT), width), LOW),
            ],
        ),
        out_shape=[jax.ShapeDtypeStruct(outputs, LOW)] * 2 + [jax.ShapeDtypeStruct(back, LOW)],
        compiler_params=ATTEND_PARAMS,
        name="attend",
    )(rows, heads, *grads)


def swap(value):
    return lax.ppermute(value, ("co", "yl"), [(0, 0), (1, 2), (2, 1), (3, 3)])


def turn(value, axis, by):
    size = lax.axis_size(axis)
    return lax.ppermute(value, axis, [(i, (i + by) % size) for i in range(size)])


def pass_kernel(*refs):
    del refs


def after(value, *earlier):
    anywhere = pl.BlockSpec(memory_space=pl.ANY)
    return pl.pallas_call(
        pass_kernel,
        in_specs=[anywhere] * (1 + len(earlier)),
        out_specs=anywhere,
        out_shape=jax.ShapeDtypeStruct(value.shape, value.dtype),
        input_output_aliases={0: 0},
        cost_estimate=SMALL,
        name="after",
    )(value, *earlier)


def live_frames(flags, count):
    frames = flags.shape[0]
    index = jnp.arange(frames, dtype=jnp.int32)
    free = flags == 0
    before = jnp.sum((index[None, :] < index[:, None]) & free[None, :], axis=1)
    hit = free[None, :] & (before[None, :] == jnp.arange(count, dtype=jnp.int32)[:, None])
    return jnp.sum(jnp.where(hit, index[None, :], 0), axis=1).astype(jnp.int32)


def pair(value, axis):
    other = turn(value, axis, 1)
    first = lax.axis_index(axis) == 0
    return jnp.concatenate([jnp.where(first, value, other), jnp.where(first, other, value)], axis=0)


def cross(value, k, back=False):
    pairs = [(co * 2 + yl, yl * 2 + (co ^ k)) for co in range(2) for yl in range(2)]
    return lax.ppermute(value, ("co", "yl"), [p[::-1] for p in pairs] if back else pairs)


def ring_gather(first, second):
    rows = first.shape[0]
    cut, more = rows // 2, second.shape[0] // 2

    def both_ways(sign):
        one = turn(first, "z", sign)
        two = turn(jnp.concatenate([one, second], axis=0), "z", sign)
        three = turn(two, "z", sign)
        four = turn(three[rows:], "z", sign)
        half, quarter = (three[cut:rows], four[more:]) if sign > 0 else (three[:cut], four[:more])
        return one, two, three, turn(half, "z", sign), four, turn(quarter, "z", sign)

    b1, b2, b3, b4, d4, d5 = both_ways(1)
    f1, f2, f3, f4, e4, e5 = both_ways(-1)
    return [first, f1, f2, f3, f4, b1, b2, b3, b4], [second, f2, f3, e4, e5, b2, b3, d4, d5]


def gather_pair(value, axis, bit):
    size = lax.axis_size(axis)
    other = lax.ppermute(value, axis, [(i, i ^ bit) for i in range(size)])
    first = lax.axis_index(axis) & bit == 0
    return jnp.concatenate([jnp.where(first, value, other), jnp.where(first, other, value)], axis=0)


def gather_rows(shard):
    return gather_pair(gather_pair(shard, "yl", 1), "yh", 1)


def gather_weight(part):
    value = gather_pair(gather_pair(part, "x", 1), "x", 2)
    value = value.reshape(4, 2, -1, part.shape[1])
    return jnp.swapaxes(value, 0, 1).reshape(-1, part.shape[1])


def scatter_sum(value, axis):
    size = lax.axis_size(axis)
    here = lax.axis_index(axis)
    total = lax.dynamic_index_in_dim(value, here, 0, keepdims=False)
    for d in range(1, size):
        part = lax.dynamic_index_in_dim(value, (here + d) % size, 0, keepdims=False)
        total = total + turn(part, axis, d)
    return total


def last_sum(value):
    here, low = lax.axis_index("yh"), lax.axis_index("yl")
    every = [(yh, co, yl) for yh in range(2) for co in range(2) for yl in range(2)]
    total = None
    for h in range(2):
        for k in range(2):
            part = lax.dynamic_index_in_dim(value, here ^ h, 0, keepdims=False)
            part = lax.dynamic_index_in_dim(part, low ^ k, 0, keepdims=False)
            moves = [
                (yh * 4 + co * 2 + yl, (yh ^ h) * 4 + (yl ^ k) * 2 + co) for yh, co, yl in every
            ]
            part = lax.ppermute(part, ("yh", "co", "yl"), moves)
            total = part if total is None else total + part
    return total


def per_device(qkv, cotangent, out_weight, gate_table, timestep, plan):
    seq = ("z", "yl")
    place = lax.axis_index("z").astype(jnp.int32)
    low = lax.axis_index("yl").astype(jnp.int32)
    frames = lax.axis_size(seq)
    tokens, dout = cotangent.shape[1:]
    live_count = frames // 4
    flags = plan[0]
    live = live_frames(flags, live_count)
    position = lax.axis_index(seq).astype(jnp.int32).reshape(1)
    qkv = jnp.transpose(qkv, (0, 2, 1, 3))

    sent_two, res_one = prepare(timestep, flags, position, qkv, cotangent, gate_table, frames)
    heads_two = lax.all_to_all(sent_two, seq, 0, 0, tiled=True)
    weight = gather_weight(gather_rows(swap(out_weight)))
    other = turn(weight, "co", 1)
    chunks = heads_two[:, 3 * tokens:][live].reshape(live_count, dout // WIDTH, -1, WIDTH)
    chunks = after(jnp.swapaxes(chunks, 1, 2).reshape(-1, dout), other)
    ring_one, ring_two = ring_gather(swap(res_one), swap(chunks))
    grads_low = project(weight, other, ring_two, lambda refs: second_pieces(refs, tokens))
    grads_low = [cross(grads_low[k], k) for k in range(2)]
    sent_one = after(split_heads(qkv, 0, frames), ring_one[4], ring_one[8], ring_two[4], ring_two[8])
    heads_one = lax.all_to_all(sent_one, seq, 0, 0, tiled=True)
    grads = project(weight, other, ring_one, first_pieces)
    grads = [cross(grads[k], k) for k in range(2)]

    rows_two = jnp.concatenate([live, place[None], low[None]])
    *out_two, back_two = attend(rows_two, heads_two, grads_low, live_count)
    grads_two = lax.all_to_all(after(back_two, heads_one, *grads), seq, 0, 0, tiled=True)
    out_two = [cross(out_two[k], k, True) for k in range(2)]

    every = jnp.arange(frames, dtype=jnp.int32)
    rows_one = jnp.concatenate([every ^ low, place[None], low[None]])
    *out_one, back_one = attend(rows_one, heads_one, grads)
    grads_one = lax.all_to_all(after(back_one, grads_two), seq, 0, 0, tiled=True)
    held = join_heads(grads_two, 1)
    out_one = [cross(out_one[k], k, True) for k in range(2)]
    out_two[0] = after(out_two[0], held)
    partial = outer([*out_one, *out_two], ring_one, ring_two)
    total = partial[0] + turn(partial[1], "co", 1)
    total = jnp.transpose(total.reshape(2, 4, 2, -1, dout), (1, 0, 2, 3, 4))
    weight_grad = last_sum(scatter_sum(total, "x"))
    result = join_heads(grads_one, 0, held)
    return jnp.transpose(result, (0, 2, 1, 3)), weight_grad


def solution(mesh):
    split = Mesh(mesh.devices.reshape(2, 4, 2, 8, 2), ("yh", "x", "co", "z", "yl"))
    dp, seq = ("yh", "x", "co"), ("z", "yl")
    placed = (
        P(None, dp + seq, None, None),
        P(None, dp + seq, None),
        P(seq + dp, None),
        P(),
        P(dp),
        P(dp, None),
    )
    return jax.shard_map(
        per_device,
        mesh=split,
        in_specs=placed,
        out_specs=(P(None, dp + seq, None, None), P(seq + dp, None)),
        check_vma=False,
    )
```

```python
import functools

import jax
import jax.numpy as jnp
from jax import lax
from jax.experimental import pallas as pl
from jax.experimental.pallas import tpu as pltpu
from jax.sharding import Mesh
from jax.sharding import PartitionSpec as P

HEAD_DIM = 64
FT = 128
KC = 1024
BLOCK = 256
WIDTH = 2 * HEAD_DIM
MIB = 1024 * 1024
PARAMS = pltpu.CompilerParams(vmem_limit_bytes=16 * MIB)
ATTEND_PARAMS = pltpu.CompilerParams(vmem_limit_bytes=20 * MIB)
RESIDENT = pl.BlockSpec(memory_space=pltpu.VMEM)
SMALL = pl.CostEstimate(flops=1000, transcendentals=0, bytes_accessed=1000)
F32 = jnp.float32
LOW = jnp.bfloat16


def prepare_kernel(time_ref, flags_ref, pos_ref, qkv_ref, cot_ref, gate_ref, sent_ref, one_ref):
    frames = sent_ref.shape[0]
    tokens, dout = one_ref.shape
    now = gate_ref[pl.ds(time_ref[0], 1), :]
    prev = gate_ref[pl.ds(time_ref[0] - 1, 1), :]
    reuse = flags_ref[pos_ref[0]].astype(F32)
    second = prev * cot_ref[1].astype(F32)
    one_ref[...] = (now * cot_ref[0].astype(F32) + reuse * second).astype(LOW)
    second = (1.0 - reuse) * second
    size = tokens // frames
    for f in range(frames):
        for w in range(3):
            sent_ref[f, w * FT:(w + 1) * FT, :] = qkv_ref[0, w, :, f * WIDTH:(f + 1) * WIDTH]
        rows = second[f * size:(f + 1) * size]
        parts = [rows[:, j * WIDTH:(j + 1) * WIDTH] for j in range(dout // WIDTH)]
        sent_ref[f, 3 * FT:, :] = jnp.concatenate(parts, axis=0).astype(LOW)


def prepare(timestep, flags, position, qkv, cotangent, gates, frames):
    _, three, tokens, inner = qkv.shape
    dout = cotangent.shape[2]
    sent = (frames, three * tokens + tokens * dout // frames // WIDTH, WIDTH)
    return pl.pallas_call(
        prepare_kernel,
        grid_spec=pltpu.PrefetchScalarGridSpec(
            num_scalar_prefetch=3,
            grid=(1,),
            in_specs=[
                pl.BlockSpec((1, three, tokens, inner), lambda *_: (1, 0, 0, 0)),
                RESIDENT,
                RESIDENT,
            ],
            out_specs=[RESIDENT, RESIDENT],
        ),
        out_shape=[
            jax.ShapeDtypeStruct(sent, LOW),
            jax.ShapeDtypeStruct((tokens, dout), LOW),
        ],
        compiler_params=PARAMS,
        cost_estimate=SMALL,
        name="prepare",
    )(timestep, flags, position, qkv, cotangent, gates)


def call_on(kernel, operands, shapes, dtype, name):
    count = len(operands)

    def body(*refs):
        kernel(refs[:count], refs[count:])

    return pl.pallas_call(
        body,
        in_specs=[RESIDENT] * count,
        out_specs=[RESIDENT] * len(shapes),
        out_shape=[jax.ShapeDtypeStruct(shape, dtype) for shape in shapes],
        compiler_params=PARAMS,
        cost_estimate=SMALL,
        name=name,
    )(*operands)


def first_pieces(refs):
    first, f1, f2, f3, f4, b1, b2, b3, b4 = refs
    rows = first.shape[0]
    far = jnp.concatenate([f4[...], b4[...]], axis=0)
    return [first[...], f1[...], f2[:rows], f3[:rows], far, b3[:rows], b2[:rows], b1[...]]


def second_pieces(refs, rows):
    second, f2, f3, f4, f5, b2, b3, b4, b5 = refs
    far = jnp.concatenate([f5[...], b5[...]], axis=0)
    return [second[...], f2[rows:], f3[rows:], f4[...], far, b4[...], b3[rows:], b2[rows:]]


def project(weight, other, ring, pieces_of):
    count, columns = ring[0].shape

    def kernel(held, outs):
        rows = jnp.concatenate([held[0][...], held[1][...]], axis=0)
        for j, piece in enumerate(pieces_of(held[2:])):
            got = lax.dot_general(piece, rows, (((1,), (1,)), ((), ())), preferred_element_type=F32)
            got = got.astype(LOW)
            for k in range(2):
                outs[k][j] = got[:, k * WIDTH:(k + 1) * WIDTH]
            outs[2][j * count:(j + 1) * count] = piece

    size = lax.axis_size("z")
    shapes = [(size, count, WIDTH)] * 2 + [(size * count, columns)]
    return call_on(kernel, [weight, other, *ring], shapes, LOW, "project")


def outer(outputs, rows_one, rows_two):
    def kernel(held, outs):
        for k in range(2):
            total = None
            for out, rows in ((held[k], held[4]), (held[2 + k], held[5])):
                left = out[...].reshape(-1, WIDTH).T
                part = jnp.dot(left, rows[...], preferred_element_type=F32)
                total = part if total is None else total + part
            outs[k][...] = total

    shape = (WIDTH, rows_one.shape[1])
    return call_on(kernel, [*outputs, rows_one, rows_two], [shape] * 2, F32, "outer")


def split_kernel(qkv_ref, sent_ref):
    for f in range(sent_ref.shape[0]):
        for w in range(3):
            sent_ref[f, w * FT:(w + 1) * FT, :] = qkv_ref[0, w, :, f * WIDTH:(f + 1) * WIDTH]


def split_heads(qkv, step, frames):
    _, three, tokens, inner = qkv.shape
    sent = (frames, three * tokens, WIDTH)
    return pl.pallas_call(
        split_kernel,
        grid=(1,),
        in_specs=[pl.BlockSpec((1, three, tokens, inner), lambda i: (step, 0, 0, 0))],
        out_specs=RESIDENT,
        out_shape=jax.ShapeDtypeStruct(sent, LOW),
        compiler_params=PARAMS,
        cost_estimate=SMALL,
        name="split_heads",
    )(qkv)


def join_kernel(back_ref, *refs):
    out_ref = refs[-1]
    for f in range(back_ref.shape[0]):
        for w in range(3):
            out_ref[0, w, :, f * WIDTH:(f + 1) * WIDTH] = back_ref[f, w * FT:(w + 1) * FT, :]


def join_heads(back, step, held=None):
    frames, rows, width = back.shape
    shape = (2, 3, rows // 3, frames * width)
    specs, operands, aliases = [RESIDENT], [back], {}
    if held is not None:
        specs.append(pl.BlockSpec(memory_space=pl.ANY))
        operands.append(held)
        aliases = {1: 0}
    return pl.pallas_call(
        join_kernel,
        grid=(1,),
        in_specs=specs,
        out_specs=pl.BlockSpec((1,) + shape[1:], lambda i: (step, 0, 0, 0)),
        out_shape=jax.ShapeDtypeStruct(shape, LOW),
        input_output_aliases=aliases,
        compiler_params=PARAMS,
        cost_estimate=SMALL,
        name="join_heads",
    )(*operands)


def live_rows(rows_ref, at, size, live, back):
    count = live * FT
    place, low = rows_ref[live], rows_ref[live + 1]
    row = lax.broadcasted_iota(jnp.int32, (size, count), 0) + at
    col = lax.broadcasted_iota(jnp.int32, (size, count), 1)
    straight, ringed = (col, row) if back else (row, col)
    part = lax.rem(ringed, 8)
    frame = lax.rem(lax.div(ringed, 8), live)
    turn_by = lax.rem(lax.div(ringed, 8 * live), 8)
    side = lax.div(ringed, 64 * live)
    eighth = lax.rem(turn_by + place, 8)
    side = side + low - 2 * side * low
    return (straight == frame * FT + eighth * 16 + side * 8 + part).astype(F32).astype(LOW)


def attend_kernel(
    rows_ref, x_ref, d_ref, f_ref, o_ref, p_ref, g_ref, dk_ref, dv_ref, kt_ref, vt_ref, s_ref, e_ref,
    all_ref, *, scale, by_frame
):
    step = pl.program_id(0)
    frames, width = x_ref.shape[0], x_ref.shape[2]
    chunks = frames * FT // KC
    per, nb = KC // FT, BLOCK // FT

    @pl.when(step == 0)
    def _():
        dk_ref[...] = jnp.zeros_like(dk_ref)
        dv_ref[...] = jnp.zeros_like(dv_ref)
        for f in range(frames):
            kt_ref[:, f * FT:(f + 1) * FT] = x_ref[f, FT:2 * FT].T
            vt_ref[:, f * FT:(f + 1) * FT] = x_ref[f, 2 * FT:3 * FT].T
            if not by_frame:
                g_ref[f, 0:FT] = jnp.zeros((FT, width), LOW)

    own = [rows_ref[step * nb + j] for j in range(nb)]
    q = jnp.concatenate([x_ref[own[j], 0:FT] for j in range(nb)], axis=0) * LOW(scale)
    if by_frame:
        do = jnp.concatenate([d_ref[0], f_ref[0]], axis=0)
    else:
        live = rows_ref.shape[0] - 2
        ringed = [r[...].reshape(-1, width) for r in (d_ref, f_ref)]
        pick = live_rows(rows_ref, step * BLOCK, BLOCK, live, False)
        do = jnp.dot(pick, jnp.concatenate(ringed, axis=0), preferred_element_type=F32).astype(LOW)
    q_t = q.T
    do_t = do.T.astype(F32)
    lane = lax.broadcasted_iota(jnp.int32, (BLOCK, width), 1)
    sub = lax.broadcasted_iota(jnp.int32, (width, BLOCK), 0)
    zero, zero_t = jnp.zeros_like(q), jnp.zeros_like(q_t)
    in_lanes = [(lane >= h * HEAD_DIM) & (lane < (h + 1) * HEAD_DIM) for h in range(2)]
    in_subs = [(sub >= h * HEAD_DIM) & (sub < (h + 1) * HEAD_DIM) for h in range(2)]

    def part_of(which, c):
        return x_ref[c * per:(c + 1) * per, which * FT:(which + 1) * FT].reshape(KC, width)

    def fold(value):
        return value.reshape(value.shape[0] // 8, 8, value.shape[1])

    deltas, scaled, outs = [], [], []
    for h in range(2):
        lo, hi = h * HEAD_DIM, (h + 1) * HEAD_DIM
        q_th = jnp.where(in_subs[h], q_t, zero_t)
        top = None
        for c in range(chunks):
            s = jnp.dot(part_of(1, c), q_th, preferred_element_type=F32)
            s_ref[h, c * KC:(c + 1) * KC, :] = s
            part = jnp.max(fold(s), axis=0)
            top = part if top is None else jnp.maximum(top, part)
        top = jnp.max(top, axis=0, keepdims=True)
        total = jnp.zeros((8, BLOCK), F32)
        out_t = jnp.zeros((HEAD_DIM, BLOCK), F32)
        for c in range(chunks):
            rows = slice(c * KC, (c + 1) * KC)
            e = jnp.exp(s_ref[h, rows, :] - top)
            total = total + jnp.sum(fold(e), axis=0)
            eb = e.astype(LOW)
            e_ref[h, rows, :] = eb
            out_t = out_t + jnp.dot(vt_ref[lo:hi, rows], eb, preferred_element_type=F32)
        inv = 1.0 / jnp.sum(total, axis=0, keepdims=True)
        out_b = (out_t * inv).astype(LOW)
        outs.append(out_b)
        part = (do_t[lo:hi] * inv).astype(LOW)
        scaled.append(part)
        deltas.append(jnp.sum(part.astype(F32) * out_b.astype(F32), axis=0, keepdims=True))
    out = jnp.concatenate(outs, axis=0).T
    if by_frame:
        o_ref[0] = out[0:FT]
        p_ref[0] = out[FT:]
    else:
        all_ref[pl.ds(pl.multiple_of(step * BLOCK, BLOCK), BLOCK), :] = out
    ds_t = jnp.concatenate(scaled, axis=0)
    ds_row = ds_t.T
    dq_t = [jnp.zeros((HEAD_DIM, BLOCK), F32) for _ in range(2)]
    d_th = [jnp.where(in_subs[h], ds_t, zero_t) for h in range(2)]
    d_row = [jnp.where(in_lanes[h], ds_row, zero) for h in range(2)]
    q_row = [jnp.where(in_lanes[h], q, zero) for h in range(2)]
    for c in range(chunks):
        rows = slice(c * KC, (c + 1) * KC)
        gs, es = [], []
        both = jnp.dot(part_of(2, c), jnp.concatenate(d_th, axis=1), preferred_element_type=F32)
        for h in range(2):
            lo, hi = h * HEAD_DIM, (h + 1) * HEAD_DIM
            dp = both[:, h * BLOCK:(h + 1) * BLOCK]
            eb = e_ref[h, rows, :]
            grad = (eb.astype(F32) * (dp - deltas[h])).astype(LOW)
            dq_t[h] = dq_t[h] + jnp.dot(kt_ref[lo:hi, rows], grad, preferred_element_type=F32)
            gs.append(grad)
            es.append(eb)
        dk = dk_ref[rows, :] + jnp.dot(jnp.concatenate(gs, axis=1), jnp.concatenate(q_row, axis=0), preferred_element_type=F32)
        dv = dv_ref[rows, :] + jnp.dot(jnp.concatenate(es, axis=1), jnp.concatenate(d_row, axis=0), preferred_element_type=F32)
        dk_ref[rows, :] = dk
        dv_ref[rows, :] = dv
    dq = (jnp.concatenate(dq_t, axis=0) * scale).astype(LOW).T
    for j in range(nb):
        g_ref[own[j], 0:FT] = dq[j * FT:(j + 1) * FT]

    @pl.when(step == pl.num_programs(0) - 1)
    def _():
        for f in range(frames):
            g_ref[f, FT:2 * FT] = dk_ref[f * FT:(f + 1) * FT, :].astype(LOW)
            g_ref[f, 2 * FT:3 * FT] = dv_ref[f * FT:(f + 1) * FT, :].astype(LOW)
        if not by_frame:
            half = live * FT // 2
            for k, ref in enumerate((o_ref, p_ref)):
                pick = live_rows(rows_ref, k * half, half, live, True)
                ringed = jnp.dot(pick, all_ref[...], preferred_element_type=F32).astype(LOW)
                ref[...] = ringed.reshape(ref.shape)


def attend(rows, heads, grads, live=0):
    frames, _, width = heads.shape
    length = frames * FT
    steps = (live or frames) * FT // BLOCK
    back = (frames, 3 * FT, width)
    outputs = grads[0].shape
    ring = outputs[0]
    if live:
        spec = RESIDENT
    else:
        spec = pl.BlockSpec(
            (1, FT, width), lambda i, r: (lax.rem(i + ring - r[frames], ring), 0, 0)
        )
    return pl.pallas_call(
        functools.partial(attend_kernel, scale=HEAD_DIM ** -0.5, by_frame=not live),
        grid_spec=pltpu.PrefetchScalarGridSpec(
            num_scalar_prefetch=1,
            grid=(steps,),
            in_specs=[RESIDENT, spec, spec],
            out_specs=[spec, spec, RESIDENT],
            scratch_shapes=[
                pltpu.VMEM((length, width), F32),
                pltpu.VMEM((length, width), F32),
                pltpu.VMEM((width, length), LOW),
                pltpu.VMEM((width, length), LOW),
                pltpu.VMEM((2, length, BLOCK), F32),
                pltpu.VMEM((2, length, BLOCK), LOW),
                pltpu.VMEM((max(live * FT, FT), width), LOW),
            ],
        ),
        out_shape=[jax.ShapeDtypeStruct(outputs, LOW)] * 2 + [jax.ShapeDtypeStruct(back, LOW)],
        compiler_params=ATTEND_PARAMS,
        name="attend",
    )(rows, heads, *grads)


def swap(value):
    return lax.ppermute(value, ("co", "yl"), [(0, 0), (1, 2), (2, 1), (3, 3)])


def turn(value, axis, by):
    size = lax.axis_size(axis)
    return lax.ppermute(value, axis, [(i, (i + by) % size) for i in range(size)])


def pass_kernel(*refs):
    del refs


def after(value, *earlier):
    anywhere = pl.BlockSpec(memory_space=pl.ANY)
    return pl.pallas_call(
        pass_kernel,
        in_specs=[anywhere] * (1 + len(earlier)),
        out_specs=anywhere,
        out_shape=jax.ShapeDtypeStruct(value.shape, value.dtype),
        input_output_aliases={0: 0},
        cost_estimate=SMALL,
        name="after",
    )(value, *earlier)


def live_frames(flags, count):
    frames = flags.shape[0]
    index = jnp.arange(frames, dtype=jnp.int32)
    free = flags == 0
    before = jnp.sum((index[None, :] < index[:, None]) & free[None, :], axis=1)
    hit = free[None, :] & (before[None, :] == jnp.arange(count, dtype=jnp.int32)[:, None])
    return jnp.sum(jnp.where(hit, index[None, :], 0), axis=1).astype(jnp.int32)


def pair(value, axis):
    other = turn(value, axis, 1)
    first = lax.axis_index(axis) == 0
    return jnp.concatenate([jnp.where(first, value, other), jnp.where(first, other, value)], axis=0)


def cross(value, k, back=False):
    pairs = [(co * 2 + yl, yl * 2 + (co ^ k)) for co in range(2) for yl in range(2)]
    return lax.ppermute(value, ("co", "yl"), [p[::-1] for p in pairs] if back else pairs)


def ring_gather(first, second):
    rows = first.shape[0]
    cut, more = rows // 2, second.shape[0] // 2

    def both_ways(sign):
        one = turn(first, "z", sign)
        two = turn(jnp.concatenate([one, second], axis=0), "z", sign)
        three = turn(two, "z", sign)
        four = turn(three[rows:], "z", sign)
        half, quarter = (three[cut:rows], four[more:]) if sign > 0 else (three[:cut], four[:more])
        return one, two, three, turn(half, "z", sign), four, turn(quarter, "z", sign)

    b1, b2, b3, b4, d4, d5 = both_ways(1)
    f1, f2, f3, f4, e4, e5 = both_ways(-1)
    return [first, f1, f2, f3, f4, b1, b2, b3, b4], [second, f2, f3, e4, e5, b2, b3, d4, d5]


def gather_pair(value, axis, bit):
    size = lax.axis_size(axis)
    other = lax.ppermute(value, axis, [(i, i ^ bit) for i in range(size)])
    first = lax.axis_index(axis) & bit == 0
    return jnp.concatenate([jnp.where(first, value, other), jnp.where(first, other, value)], axis=0)


def gather_rows(shard):
    return gather_pair(gather_pair(shard, "yl", 1), "yh", 1)


def gather_weight(part):
    value = gather_pair(gather_pair(part, "x", 1), "x", 2)
    value = value.reshape(4, 2, -1, part.shape[1])
    return jnp.swapaxes(value, 0, 1).reshape(-1, part.shape[1])


def scatter_sum(value, axis):
    size = lax.axis_size(axis)
    here = lax.axis_index(axis)
    total = lax.dynamic_index_in_dim(value, here, 0, keepdims=False)
    for d in range(1, size):
        part = lax.dynamic_index_in_dim(value, (here + d) % size, 0, keepdims=False)
        total = total + turn(part, axis, d)
    return total


def last_sum(value):
    here, low = lax.axis_index("yh"), lax.axis_index("yl")
    every = [(yh, co, yl) for yh in range(2) for co in range(2) for yl in range(2)]
    total = None
    for h in range(2):
        for k in range(2):
            part = lax.dynamic_index_in_dim(value, here ^ h, 0, keepdims=False)
            part = lax.dynamic_index_in_dim(part, low ^ k, 0, keepdims=False)
            moves = [
                (yh * 4 + co * 2 + yl, (yh ^ h) * 4 + (yl ^ k) * 2 + co) for yh, co, yl in every
            ]
            part = lax.ppermute(part, ("yh", "co", "yl"), moves)
            total = part if total is None else total + part
    return total


def per_device(qkv, cotangent, out_weight, gate_table, timestep, plan):
    seq = ("z", "yl")
    place = lax.axis_index("z").astype(jnp.int32)
    low = lax.axis_index("yl").astype(jnp.int32)
    frames = lax.axis_size(seq)
    tokens, dout = cotangent.shape[1:]
    live_count = frames // 4
    flags = plan[0]
    live = live_frames(flags, live_count)
    position = lax.axis_index(seq).astype(jnp.int32).reshape(1)
    qkv = jnp.transpose(qkv, (0, 2, 1, 3))

    sent_two, res_one = prepare(timestep, flags, position, qkv, cotangent, gate_table, frames)
    heads_two = lax.all_to_all(sent_two, seq, 0, 0, tiled=True)
    weight = gather_weight(gather_rows(swap(out_weight)))
    other = turn(weight, "co", 1)
    chunks = heads_two[:, 3 * tokens:][live].reshape(live_count, dout // WIDTH, -1, WIDTH)
    chunks = swap(jnp.swapaxes(chunks, 1, 2).reshape(-1, dout))
    ring_one, ring_two = ring_gather(swap(res_one), after(chunks, other))
    *grads_low, rows_low = project(
        weight, other, ring_two, lambda refs: second_pieces(refs, tokens)
    )
    grads_low = [cross(grads_low[k], k) for k in range(2)]
    sent_one = after(split_heads(qkv, 0, frames), ring_one[4], ring_one[8], *grads_low)
    heads_one = lax.all_to_all(sent_one, seq, 0, 0, tiled=True)
    *grads, rows_high = project(weight, other, ring_one, first_pieces)
    grads = [cross(grads[k], k) for k in range(2)]

    rows_two = jnp.concatenate([live, place[None], low[None]])
    *out_two, back_two = attend(rows_two, heads_two, grads_low, live_count)
    grads_two = lax.all_to_all(after(back_two, *grads), seq, 0, 0, tiled=True)
    out_two = [cross(out_two[k], k, True) for k in range(2)]

    every = jnp.arange(frames, dtype=jnp.int32)
    rows_one = jnp.concatenate([every ^ low, place[None], low[None]])
    *out_one, back_one = attend(rows_one, heads_one, grads)
    grads_one = lax.all_to_all(after(back_one, grads_two), seq, 0, 0, tiled=True)
    held = join_heads(grads_two, 1)
    out_one = [cross(out_one[k], k, True) for k in range(2)]
    out_two[0] = after(out_two[0], held)
    partial = outer([*out_one, *out_two], rows_high, rows_low)
    total = partial[0] + turn(partial[1], "co", 1)
    total = jnp.transpose(total.reshape(2, 4, 2, -1, dout), (1, 0, 2, 3, 4))
    weight_grad = last_sum(scatter_sum(total, "x"))
    result = join_heads(grads_one, 0, held)
    return jnp.transpose(result, (0, 2, 1, 3)), weight_grad


def solution(mesh):
    split = Mesh(mesh.devices.reshape(2, 4, 2, 8, 2), ("yh", "x", "co", "z", "yl"))
    dp, seq = ("yh", "x", "co"), ("z", "yl")
    placed = (
        P(None, dp + seq, None, None),
        P(None, dp + seq, None),
        P(seq + dp, None),
        P(),
        P(dp),
        P(dp, None),
    )
    return jax.shard_map(
        per_device,
        mesh=split,
        in_specs=placed,
        out_specs=(P(None, dp + seq, None, None), P(seq + dp, None)),
        check_vma=False,
    )
```

```python
import functools

import jax
import jax.numpy as jnp
from jax import lax
from jax.experimental import pallas as pl
from jax.experimental.pallas import tpu as pltpu
from jax.sharding import Mesh
from jax.sharding import PartitionSpec as P

HEAD_DIM = 64
FT = 128
KC = 1024
BLOCK = 256
WIDTH = 2 * HEAD_DIM
MIB = 1024 * 1024
PARAMS = pltpu.CompilerParams(vmem_limit_bytes=16 * MIB)
ATTEND_PARAMS = pltpu.CompilerParams(vmem_limit_bytes=20 * MIB)
RESIDENT = pl.BlockSpec(memory_space=pltpu.VMEM)
SMALL = pl.CostEstimate(flops=1000, transcendentals=0, bytes_accessed=1000)
F32 = jnp.float32
LOW = jnp.bfloat16


def prepare_kernel(time_ref, flags_ref, pos_ref, qkv_ref, cot_ref, gate_ref, sent_ref, one_ref):
    frames = sent_ref.shape[0]
    tokens, dout = one_ref.shape
    now = gate_ref[pl.ds(time_ref[0], 1), :]
    prev = gate_ref[pl.ds(time_ref[0] - 1, 1), :]
    reuse = flags_ref[pos_ref[0]].astype(F32)
    second = prev * cot_ref[1].astype(F32)
    one_ref[...] = (now * cot_ref[0].astype(F32) + reuse * second).astype(LOW)
    second = (1.0 - reuse) * second
    size = tokens // frames
    for f in range(frames):
        for w in range(3):
            sent_ref[f, w * FT:(w + 1) * FT, :] = qkv_ref[0, w, :, f * WIDTH:(f + 1) * WIDTH]
        rows = second[f * size:(f + 1) * size]
        parts = [rows[:, j * WIDTH:(j + 1) * WIDTH] for j in range(dout // WIDTH)]
        sent_ref[f, 3 * FT:, :] = jnp.concatenate(parts, axis=0).astype(LOW)


def prepare(timestep, flags, position, qkv, cotangent, gates, frames):
    _, three, tokens, inner = qkv.shape
    dout = cotangent.shape[2]
    sent = (frames, three * tokens + tokens * dout // frames // WIDTH, WIDTH)
    return pl.pallas_call(
        prepare_kernel,
        grid_spec=pltpu.PrefetchScalarGridSpec(
            num_scalar_prefetch=3,
            grid=(1,),
            in_specs=[
                pl.BlockSpec((1, three, tokens, inner), lambda *_: (1, 0, 0, 0)),
                RESIDENT,
                RESIDENT,
            ],
            out_specs=[RESIDENT, RESIDENT],
        ),
        out_shape=[
            jax.ShapeDtypeStruct(sent, LOW),
            jax.ShapeDtypeStruct((tokens, dout), LOW),
        ],
        compiler_params=PARAMS,
        cost_estimate=SMALL,
        name="prepare",
    )(timestep, flags, position, qkv, cotangent, gates)


def call_on(kernel, operands, shapes, dtype, name):
    count = len(operands)

    def body(*refs):
        kernel(refs[:count], refs[count:])

    return pl.pallas_call(
        body,
        in_specs=[RESIDENT] * count,
        out_specs=[RESIDENT] * len(shapes),
        out_shape=[jax.ShapeDtypeStruct(shape, dtype) for shape in shapes],
        compiler_params=PARAMS,
        cost_estimate=SMALL,
        name=name,
    )(*operands)


def first_pieces(refs):
    first, f1, f2, f3, f4, b1, b2, b3, b4 = refs
    rows = first.shape[0]
    far = jnp.concatenate([f4[...], b4[...]], axis=0)
    return [first[...], f1[...], f2[:rows], f3[:rows], far, b3[:rows], b2[:rows], b1[...]]


def second_pieces(refs, rows):
    second, f2, f3, f4, f5, b2, b3, b4, b5 = refs
    far = jnp.concatenate([f5[...], b5[...]], axis=0)
    return [second[...], f2[rows:], f3[rows:], f4[...], far, b4[...], b3[rows:], b2[rows:]]


def project(weight, other, ring, pieces_of):
    count, columns = ring[0].shape

    def kernel(held, outs):
        rows = jnp.concatenate([held[0][...], held[1][...]], axis=0)
        for j, piece in enumerate(pieces_of(held[2:])):
            got = lax.dot_general(piece, rows, (((1,), (1,)), ((), ())), preferred_element_type=F32)
            got = got.astype(LOW)
            for k in range(2):
                outs[k][j] = got[:, k * WIDTH:(k + 1) * WIDTH]
            outs[2][j * count:(j + 1) * count] = piece

    size = lax.axis_size("z")
    shapes = [(size, count, WIDTH)] * 2 + [(size * count, columns)]
    return call_on(kernel, [weight, other, *ring], shapes, LOW, "project")


def outer(outputs, rows_one, rows_two):
    def kernel(held, outs):
        for k in range(2):
            total = None
            for out, rows in ((held[k], held[4]), (held[2 + k], held[5])):
                left = out[...].reshape(-1, WIDTH).T
                part = jnp.dot(left, rows[...], preferred_element_type=F32)
                total = part if total is None else total + part
            outs[k][...] = total

    shape = (WIDTH, rows_one.shape[1])
    return call_on(kernel, [*outputs, rows_one, rows_two], [shape] * 2, F32, "outer")


def split_kernel(qkv_ref, sent_ref):
    for f in range(sent_ref.shape[0]):
        for w in range(3):
            sent_ref[f, w * FT:(w + 1) * FT, :] = qkv_ref[0, w, :, f * WIDTH:(f + 1) * WIDTH]


def split_heads(qkv, step, frames):
    _, three, tokens, inner = qkv.shape
    sent = (frames, three * tokens, WIDTH)
    return pl.pallas_call(
        split_kernel,
        grid=(1,),
        in_specs=[pl.BlockSpec((1, three, tokens, inner), lambda i: (step, 0, 0, 0))],
        out_specs=RESIDENT,
        out_shape=jax.ShapeDtypeStruct(sent, LOW),
        compiler_params=PARAMS,
        cost_estimate=SMALL,
        name="split_heads",
    )(qkv)


def join_kernel(back_ref, *refs):
    out_ref = refs[-1]
    for f in range(back_ref.shape[0]):
        for w in range(3):
            out_ref[0, w, :, f * WIDTH:(f + 1) * WIDTH] = back_ref[f, w * FT:(w + 1) * FT, :]


def join_heads(back, step, held=None):
    frames, rows, width = back.shape
    shape = (2, 3, rows // 3, frames * width)
    specs, operands, aliases = [RESIDENT], [back], {}
    if held is not None:
        specs.append(pl.BlockSpec(memory_space=pl.ANY))
        operands.append(held)
        aliases = {1: 0}
    return pl.pallas_call(
        join_kernel,
        grid=(1,),
        in_specs=specs,
        out_specs=pl.BlockSpec((1,) + shape[1:], lambda i: (step, 0, 0, 0)),
        out_shape=jax.ShapeDtypeStruct(shape, LOW),
        input_output_aliases=aliases,
        compiler_params=PARAMS,
        cost_estimate=SMALL,
        name="join_heads",
    )(*operands)


def live_rows(rows_ref, at, size, live, back):
    count = live * FT
    place, low = rows_ref[live], rows_ref[live + 1]
    row = lax.broadcasted_iota(jnp.int32, (size, count), 0) + at
    col = lax.broadcasted_iota(jnp.int32, (size, count), 1)
    straight, ringed = (col, row) if back else (row, col)
    part = lax.rem(ringed, 8)
    frame = lax.rem(lax.div(ringed, 8), live)
    turn_by = lax.rem(lax.div(ringed, 8 * live), 8)
    side = lax.div(ringed, 64 * live)
    eighth = lax.rem(turn_by + place, 8)
    side = side + low - 2 * side * low
    return (straight == frame * FT + eighth * 16 + side * 8 + part).astype(F32).astype(LOW)


def attend_kernel(
    rows_ref, x_ref, d_ref, f_ref, o_ref, p_ref, g_ref, dk_ref, dv_ref, kt_ref, vt_ref, s_ref, e_ref,
    all_ref, *, scale, by_frame
):
    step = pl.program_id(0)
    frames, width = x_ref.shape[0], x_ref.shape[2]
    chunks = frames * FT // KC
    per, nb = KC // FT, BLOCK // FT

    @pl.when(step == 0)
    def _():
        dk_ref[...] = jnp.zeros_like(dk_ref)
        dv_ref[...] = jnp.zeros_like(dv_ref)
        for f in range(frames):
            kt_ref[:, f * FT:(f + 1) * FT] = x_ref[f, FT:2 * FT].T
            vt_ref[:, f * FT:(f + 1) * FT] = x_ref[f, 2 * FT:3 * FT].T
            if not by_frame:
                g_ref[f, 0:FT] = jnp.zeros((FT, width), LOW)

    own = [rows_ref[step * nb + j] for j in range(nb)]
    q = jnp.concatenate([x_ref[own[j], 0:FT] for j in range(nb)], axis=0) * LOW(scale)
    if by_frame:
        do = jnp.concatenate([d_ref[0], f_ref[0]], axis=0)
    else:
        live = rows_ref.shape[0] - 2
        ringed = [r[...].reshape(-1, width) for r in (d_ref, f_ref)]
        pick = live_rows(rows_ref, step * BLOCK, BLOCK, live, False)
        do = jnp.dot(pick, jnp.concatenate(ringed, axis=0), preferred_element_type=F32).astype(LOW)
    q_t = q.T
    do_t = do.T.astype(F32)
    lane = lax.broadcasted_iota(jnp.int32, (BLOCK, width), 1)
    sub = lax.broadcasted_iota(jnp.int32, (width, BLOCK), 0)
    zero, zero_t = jnp.zeros_like(q), jnp.zeros_like(q_t)
    in_lanes = [(lane >= h * HEAD_DIM) & (lane < (h + 1) * HEAD_DIM) for h in range(2)]
    in_subs = [(sub >= h * HEAD_DIM) & (sub < (h + 1) * HEAD_DIM) for h in range(2)]

    def part_of(which, c):
        return x_ref[c * per:(c + 1) * per, which * FT:(which + 1) * FT].reshape(KC, width)

    def fold(value):
        return value.reshape(value.shape[0] // 8, 8, value.shape[1])

    deltas, scaled, outs = [], [], []
    for h in range(2):
        lo, hi = h * HEAD_DIM, (h + 1) * HEAD_DIM
        q_th = jnp.where(in_subs[h], q_t, zero_t)
        top = None
        for c in range(chunks):
            s = jnp.dot(part_of(1, c), q_th, preferred_element_type=F32)
            s_ref[h, c * KC:(c + 1) * KC, :] = s
            part = jnp.max(fold(s), axis=0)
            top = part if top is None else jnp.maximum(top, part)
        top = jnp.max(top, axis=0, keepdims=True)
        total = jnp.zeros((8, BLOCK), F32)
        out_t = jnp.zeros((HEAD_DIM, BLOCK), F32)
        for c in range(chunks):
            rows = slice(c * KC, (c + 1) * KC)
            e = jnp.exp(s_ref[h, rows, :] - top)
            total = total + jnp.sum(fold(e), axis=0)
            eb = e.astype(LOW)
            e_ref[h, rows, :] = eb
            out_t = out_t + jnp.dot(vt_ref[lo:hi, rows], eb, preferred_element_type=F32)
        inv = 1.0 / jnp.sum(total, axis=0, keepdims=True)
        out_b = (out_t * inv).astype(LOW)
        outs.append(out_b)
        part = (do_t[lo:hi] * inv).astype(LOW)
        scaled.append(part)
        deltas.append(jnp.sum(part.astype(F32) * out_b.astype(F32), axis=0, keepdims=True))
    out = jnp.concatenate(outs, axis=0).T
    if by_frame:
        o_ref[0] = out[0:FT]
        p_ref[0] = out[FT:]
    else:
        all_ref[pl.ds(pl.multiple_of(step * BLOCK, BLOCK), BLOCK), :] = out
    ds_t = jnp.concatenate(scaled, axis=0)
    ds_row = ds_t.T
    dq_t = [jnp.zeros((HEAD_DIM, BLOCK), F32) for _ in range(2)]
    d_th = [jnp.where(in_subs[h], ds_t, zero_t) for h in range(2)]
    d_row = [jnp.where(in_lanes[h], ds_row, zero) for h in range(2)]
    q_row = [jnp.where(in_lanes[h], q, zero) for h in range(2)]
    for c in range(chunks):
        rows = slice(c * KC, (c + 1) * KC)
        gs, es = [], []
        both = jnp.dot(part_of(2, c), jnp.concatenate(d_th, axis=1), preferred_element_type=F32)
        for h in range(2):
            lo, hi = h * HEAD_DIM, (h + 1) * HEAD_DIM
            dp = both[:, h * BLOCK:(h + 1) * BLOCK]
            eb = e_ref[h, rows, :]
            grad = (eb.astype(F32) * (dp - deltas[h])).astype(LOW)
            dq_t[h] = dq_t[h] + jnp.dot(kt_ref[lo:hi, rows], grad, preferred_element_type=F32)
            gs.append(grad)
            es.append(eb)
        dk = dk_ref[rows, :] + jnp.dot(jnp.concatenate(gs, axis=1), jnp.concatenate(q_row, axis=0), preferred_element_type=F32)
        dv = dv_ref[rows, :] + jnp.dot(jnp.concatenate(es, axis=1), jnp.concatenate(d_row, axis=0), preferred_element_type=F32)
        dk_ref[rows, :] = dk
        dv_ref[rows, :] = dv
    dq = (jnp.concatenate(dq_t, axis=0) * scale).astype(LOW).T
    for j in range(nb):
        g_ref[own[j], 0:FT] = dq[j * FT:(j + 1) * FT]

    @pl.when(step == pl.num_programs(0) - 1)
    def _():
        for f in range(frames):
            g_ref[f, FT:2 * FT] = dk_ref[f * FT:(f + 1) * FT, :].astype(LOW)
            g_ref[f, 2 * FT:3 * FT] = dv_ref[f * FT:(f + 1) * FT, :].astype(LOW)
        if not by_frame:
            half = live * FT // 2
            for k, ref in enumerate((o_ref, p_ref)):
                pick = live_rows(rows_ref, k * half, half, live, True)
                ringed = jnp.dot(pick, all_ref[...], preferred_element_type=F32).astype(LOW)
                ref[...] = ringed.reshape(ref.shape)


def attend(rows, heads, grads, live=0):
    frames, _, width = heads.shape
    length = frames * FT
    steps = (live or frames) * FT // BLOCK
    back = (frames, 3 * FT, width)
    outputs = grads[0].shape
    ring = outputs[0]
    if live:
        spec = RESIDENT
    else:
        spec = pl.BlockSpec(
            (1, FT, width), lambda i, r: (lax.rem(i + ring - r[frames], ring), 0, 0)
        )
    return pl.pallas_call(
        functools.partial(attend_kernel, scale=HEAD_DIM ** -0.5, by_frame=not live),
        grid_spec=pltpu.PrefetchScalarGridSpec(
            num_scalar_prefetch=1,
            grid=(steps,),
            in_specs=[RESIDENT, spec, spec],
            out_specs=[spec, spec, RESIDENT],
            scratch_shapes=[
                pltpu.VMEM((length, width), F32),
                pltpu.VMEM((length, width), F32),
                pltpu.VMEM((width, length), LOW),
                pltpu.VMEM((width, length), LOW),
                pltpu.VMEM((2, length, BLOCK), F32),
                pltpu.VMEM((2, length, BLOCK), LOW),
                pltpu.VMEM((max(live * FT, FT), width), LOW),
            ],
        ),
        out_shape=[jax.ShapeDtypeStruct(outputs, LOW)] * 2 + [jax.ShapeDtypeStruct(back, LOW)],
        compiler_params=ATTEND_PARAMS,
        name="attend",
    )(rows, heads, *grads)


def swap(value):
    return lax.ppermute(value, ("co", "yl"), [(0, 0), (1, 2), (2, 1), (3, 3)])


def turn(value, axis, by):
    size = lax.axis_size(axis)
    return lax.ppermute(value, axis, [(i, (i + by) % size) for i in range(size)])


def pass_kernel(*refs):
    del refs


def after(value, *earlier):
    anywhere = pl.BlockSpec(memory_space=pl.ANY)
    return pl.pallas_call(
        pass_kernel,
        in_specs=[anywhere] * (1 + len(earlier)),
        out_specs=anywhere,
        out_shape=jax.ShapeDtypeStruct(value.shape, value.dtype),
        input_output_aliases={0: 0},
        cost_estimate=SMALL,
        name="after",
    )(value, *earlier)


def live_frames(flags, count):
    frames = flags.shape[0]
    index = jnp.arange(frames, dtype=jnp.int32)
    free = flags == 0
    before = jnp.sum((index[None, :] < index[:, None]) & free[None, :], axis=1)
    hit = free[None, :] & (before[None, :] == jnp.arange(count, dtype=jnp.int32)[:, None])
    return jnp.sum(jnp.where(hit, index[None, :], 0), axis=1).astype(jnp.int32)


def pair(value, axis):
    other = turn(value, axis, 1)
    first = lax.axis_index(axis) == 0
    return jnp.concatenate([jnp.where(first, value, other), jnp.where(first, other, value)], axis=0)


def cross(value, k, back=False):
    pairs = [(co * 2 + yl, yl * 2 + (co ^ k)) for co in range(2) for yl in range(2)]
    return lax.ppermute(value, ("co", "yl"), [p[::-1] for p in pairs] if back else pairs)


def ring_gather(first, second):
    rows = first.shape[0]
    cut, more = rows // 2, second.shape[0] // 2

    def both_ways(sign):
        one = turn(first, "z", sign)
        two = turn(jnp.concatenate([one, second], axis=0), "z", sign)
        three = turn(two, "z", sign)
        four = turn(three[rows:], "z", sign)
        half, quarter = (three[cut:rows], four[more:]) if sign > 0 else (three[:cut], four[:more])
        return one, two, three, turn(half, "z", sign), four, turn(quarter, "z", sign)

    b1, b2, b3, b4, d4, d5 = both_ways(1)
    f1, f2, f3, f4, e4, e5 = both_ways(-1)
    return [first, f1, f2, f3, f4, b1, b2, b3, b4], [second, f2, f3, e4, e5, b2, b3, d4, d5]


def gather_pair(value, axis, bit):
    size = lax.axis_size(axis)
    other = lax.ppermute(value, axis, [(i, i ^ bit) for i in range(size)])
    first = lax.axis_index(axis) & bit == 0
    return jnp.concatenate([jnp.where(first, value, other), jnp.where(first, other, value)], axis=0)


def gather_rows(shard):
    return gather_pair(gather_pair(shard, "yl", 1), "yh", 1)


def gather_weight(part):
    value = gather_pair(gather_pair(part, "x", 1), "x", 2)
    value = value.reshape(4, 2, -1, part.shape[1])
    return jnp.swapaxes(value, 0, 1).reshape(-1, part.shape[1])


def scatter_sum(value, axis):
    size = lax.axis_size(axis)
    here = lax.axis_index(axis)
    total = lax.dynamic_index_in_dim(value, here, 0, keepdims=False)
    for d in range(1, size):
        part = lax.dynamic_index_in_dim(value, (here + d) % size, 0, keepdims=False)
        total = total + turn(part, axis, d)
    return total


def last_sum(value):
    here, low = lax.axis_index("yh"), lax.axis_index("yl")
    every = [(yh, co, yl) for yh in range(2) for co in range(2) for yl in range(2)]
    total = None
    for h in range(2):
        for k in range(2):
            part = lax.dynamic_index_in_dim(value, here ^ h, 0, keepdims=False)
            part = lax.dynamic_index_in_dim(part, low ^ k, 0, keepdims=False)
            moves = [
                (yh * 4 + co * 2 + yl, (yh ^ h) * 4 + (yl ^ k) * 2 + co) for yh, co, yl in every
            ]
            part = lax.ppermute(part, ("yh", "co", "yl"), moves)
            total = part if total is None else total + part
    return total


def per_device(qkv, cotangent, out_weight, gate_table, timestep, plan):
    seq = ("z", "yl")
    place = lax.axis_index("z").astype(jnp.int32)
    low = lax.axis_index("yl").astype(jnp.int32)
    frames = lax.axis_size(seq)
    tokens, dout = cotangent.shape[1:]
    live_count = frames // 4
    flags = plan[0]
    live = live_frames(flags, live_count)
    position = lax.axis_index(seq).astype(jnp.int32).reshape(1)
    qkv = jnp.transpose(qkv, (0, 2, 1, 3))

    sent_two, res_one = prepare(timestep, flags, position, qkv, cotangent, gate_table, frames)
    heads_two = lax.all_to_all(sent_two, seq, 0, 0, tiled=True)
    weight = gather_weight(gather_rows(swap(out_weight)))
    other = turn(weight, "co", 1)
    chunks = heads_two[:, 3 * tokens:][live].reshape(live_count, dout // WIDTH, -1, WIDTH)
    chunks = swap(jnp.swapaxes(chunks, 1, 2).reshape(-1, dout))
    ring_one, ring_two = ring_gather(swap(res_one), after(chunks, other))
    *grads_low, rows_low = project(
        weight, other, ring_two, lambda refs: second_pieces(refs, tokens)
    )
    grads_low = [cross(grads_low[k], k) for k in range(2)]
    sent_one = after(split_heads(qkv, 0, frames), ring_one[4], ring_one[8], *grads_low)
    heads_one = lax.all_to_all(sent_one, seq, 0, 0, tiled=True)
    *high_here, rows_high = project(weight, other, ring_one, first_pieces)
    grads = [cross(high_here[k], k) for k in range(2)]

    rows_two = jnp.concatenate([live, place[None], low[None]])
    *out_two, back_two = attend(rows_two, heads_two, grads_low, live_count)
    grads_two = lax.all_to_all(after(back_two, *high_here), seq, 0, 0, tiled=True)
    out_two = [cross(out_two[k], k, True) for k in range(2)]

    every = jnp.arange(frames, dtype=jnp.int32)
    rows_one = jnp.concatenate([every ^ low, place[None], low[None]])
    *out_one, back_one = attend(rows_one, heads_one, grads)
    grads_one = lax.all_to_all(after(back_one, grads_two), seq, 0, 0, tiled=True)
    held = join_heads(grads_two, 1)
    out_one = [cross(out_one[k], k, True) for k in range(2)]
    out_two[0] = after(out_two[0], held)
    partial = outer([*out_one, *out_two], rows_high, rows_low)
    total = partial[0] + turn(partial[1], "co", 1)
    total = jnp.transpose(total.reshape(2, 4, 2, -1, dout), (1, 0, 2, 3, 4))
    weight_grad = last_sum(scatter_sum(total, "x"))
    result = join_heads(grads_one, 0, held)
    return jnp.transpose(result, (0, 2, 1, 3)), weight_grad


def solution(mesh):
    split = Mesh(mesh.devices.reshape(2, 4, 2, 8, 2), ("yh", "x", "co", "z", "yl"))
    dp, seq = ("yh", "x", "co"), ("z", "yl")
    placed = (
        P(None, dp + seq, None, None),
        P(None, dp + seq, None),
        P(seq + dp, None),
        P(),
        P(dp),
        P(dp, None),
    )
    return jax.shard_map(
        per_device,
        mesh=split,
        in_specs=placed,
        out_specs=(P(None, dp + seq, None, None), P(seq + dp, None)),
        check_vma=False,
    )
```
